768 devices in a mesh: outer: 4 (over x_hi, core), rep: 16 (over y, x_lo), exp: 12 (over z).
Axes of the slice: x: 4 (x_hi: 2, x_lo: 2; x = x_hi * 2 + x_lo), y: 8, z: 12, core: 2. Of those that a mesh axis runs over, the one named last changes fastest.
Arguments:
- saved_hidden: bfloat16 [4, 16, 4608, 512], P('outer', 'rep', 'exp'), may hold values from -6 to 6
- routed_grad: bfloat16 [4, 16, 4608, 2048], P('outer', 'rep', 'exp'), may hold values from -0.19921875 to 0.19921875
- expert_counts: int32 [4, 16, 24], P('outer', 'rep', 'exp'), may hold values from 0 to 384, as said below
- block_starts: int32 [4, 16, 24], P('outer', 'rep', 'exp'), may hold values from 0 to 3
- master_weights: float32 [24, 2048, 512], P('exp', 'rep', 'outer'), may hold values from -0.0125 to 0.0125
- first_moment: float32 [24, 2048, 512], P('exp', 'rep', 'outer'), may hold values from -0.9 to 0.9
- second_moment: float32 [24, 2048, 512], P('exp', 'rep', 'outer'), may hold values from 0.01 to 1
Outputs:
- new_master: float32 [24, 2048, 512], P('exp', 'rep', 'outer')
- new_first: float32 [24, 2048, 512], P('exp', 'rep', 'outer')
- new_second: float32 [24, 2048, 512], P('exp', 'rep', 'outer')
- new_weights: bfloat16 [24, 2048, 512], P('exp')
The draws below stay inside these ranges and needn't reach their ends.
Inputs may be any that keep to these rules, and one draw needn't show every extreme that they name: On each device, the rows of its local expert e are rows 128 * block_starts[e] to 128 * block_starts[e] + expert_counts[e] - 1 of its 384 expert-side rows; the local experts come in increasing order of e, each in whole blocks of 128 rows of its own that no other expert touches, all within the device's 3 blocks; other rows belong to no expert. In every draw some device gives all its 3 blocks to one expert.
All inputs are finite; a program needn't handle non-finite values.
Results may differ from the reference program's by a relative error of at most 0.015.
Values may be sent and summed in bfloat16 or wider, within the bound.
A program may use at most 32 MiB of HBM per device.

```python
import math
import jax
import jax.numpy as jnp
from jax import lax

D = 2048
FF = 512
EXP_DEV = 2
CAP = 32
BLOCK = 128
EXPERTS = 24
N_OUTER = 4
N_REP = 16
N_EXP = 12


def expert_layout(key):
    block_total = N_EXP * CAP // BLOCK
    key_raw, key_gap, key_extra = jax.random.split(jax.random.fold_in(key, 7), 3)
    shape = (N_OUTER, N_REP, N_EXP, EXP_DEV)
    base = jax.random.randint(key_raw, shape, 0, 4)
    weights_raw = base * base
    summed = jnp.sum(weights_raw, axis=-1, keepdims=True)
    blocks_each = weights_raw * block_total // jnp.maximum(summed, 9)
    leading = jnp.zeros((EXP_DEV,), jnp.int32).at[0].set(block_total)
    blocks_each = blocks_each.at[0, 0, 0].set(leading)
    slack = block_total - jnp.sum(blocks_each, axis=-1, keepdims=True)
    gap_raw = jax.random.randint(key_gap, shape, 0, 4)
    gaps = gap_raw * slack // jnp.maximum(jnp.sum(gap_raw, axis=-1, keepdims=True), 1)
    starts = jnp.cumsum(gaps + blocks_each, axis=-1) - blocks_each
    extra = jax.random.randint(key_extra, shape, 0, BLOCK)
    extra = extra.at[0, 0, 0, 0].set(BLOCK - 1)
    counts = jnp.where(blocks_each > 0, (blocks_each - 1) * BLOCK + 1 + extra, 0)
    counts = counts.reshape(N_OUTER, N_REP, N_EXP * EXP_DEV).astype(jnp.int32)
    starts = starts.reshape(N_OUTER, N_REP, N_EXP * EXP_DEV).astype(jnp.int32)
    return (counts, starts)


def draw_expert_counts(key, part):
    return expert_layout(key)[0]


def draw_block_starts(key, part):
    return expert_layout(key)[1]


def raised(array, stream_key, source, target, blocks, factor):
    def block_of(axis_at):
        return (jnp.arange(array.shape[axis_at]) // (array.shape[axis_at] // blocks)).reshape((-1,) + (1,) * (array.ndim - 1 - axis_at))

    near = jax.random.permutation(stream_key, blocks)[block_of(target)]
    second = (block_of(target) + blocks // 2) % blocks
    return jnp.where((block_of(source) == near) | (block_of(source) == second), factor * array, array)


def block_scale(rng, extent, shards, least, largest):
    def one(dim, blocks):
        heights = jax.random.uniform(jax.random.fold_in(jax.random.fold_in(rng, 6), dim), (blocks,), jnp.float32, least / len(shards), largest / len(shards))
        return jnp.repeat(jnp.exp(heights), extent[dim] // blocks).reshape((-1,) + (1,) * (len(extent) - dim - 1))

    gain = one(*shards[0])
    for cut in shards[1:]:
        gain = gain * one(*cut)
    return gain


def centred(key, extent, spread, reach, shards=(), kind=jnp.bfloat16):
    factor_of = block_scale(key, extent, shards, -0.22, 0.18) if shards else 1.0
    result = jax.random.normal(key, extent, jnp.float32) * spread * factor_of
    return jnp.minimum(jnp.maximum(result, -reach), reach).astype(kind)


def bell_draw_with(own_key, extent, spread, limit, pieces, heavy, held_as=jnp.bfloat16):
    array = spread * jax.random.normal(own_key, extent, jnp.float32)
    if pieces:
        array = array * block_scale(own_key, extent, pieces, -0.22, 0.18)
    return jnp.clip(raised(array, jax.random.fold_in(own_key, 3), *heavy), -limit, limit).astype(held_as)


def setup_inputs(seed: int = 0) -> dict:
    splits = jax.random.split(jax.random.key(seed), 8)
    return {
        "saved_hidden": centred(splits[0], (N_OUTER, N_REP, N_EXP * N_EXP * CAP, FF), 1.0, 6.0, ((0, 4), (1, 16), (2, 12))),
        "routed_grad": bell_draw_with(splits[1], (N_OUTER, N_REP, N_EXP * N_EXP * CAP, D), 0.03125, 0.19921875, ((0, 4), (1, 16), (2, 12)), (1, 3, 16, 2.0)),
        "expert_counts": draw_expert_counts(jax.random.fold_in(splits[7], 71), 0),
        "block_starts": draw_block_starts(jax.random.fold_in(splits[7], 71), 0),
        "master_weights": centred(splits[4], (EXPERTS, D, FF), 0.005, 0.0125, ((0, 12), (1, 16), (2, 4)), jnp.float32),
        "first_moment": centred(splits[5], (EXPERTS, D, FF), 0.15, 0.9, ((0, 12), (1, 16), (2, 4)), jnp.float32),
        "second_moment": jnp.clip(jnp.exp(math.log(1.0) - 4.6051702 * jax.random.uniform(splits[6], (EXPERTS, D, FF), jnp.float32) ** block_scale(splits[6], (EXPERTS, D, FF), ((0, 12), (1, 16), (2, 4)), -0.2, 0.2)), 0.01, 1.0),
    }


beta_one = 0.9
beta_two = 0.95
learn_rate = 0.001
decay_rate = 0.1
epsilon = 1e-08
correct_one = 0.9999734386011124
correct_two = 0.994079470779666

def adamw(grad_part, master, moment_one, moment_two):
    new_one = beta_one * moment_one + (1.0 - beta_one) * grad_part
    new_two = beta_two * moment_two + (1.0 - beta_two) * grad_part * grad_part
    update = new_one / correct_one / (jnp.sqrt(new_two / correct_two) + epsilon)
    new_master = master - learn_rate * (update + decay_rate * master)
    return (new_master, new_one, new_two)

def device_partial(hidden, grads, counts, starts):
    positions = jnp.arange(hidden.shape[0], dtype=jnp.int32)
    lower_row = starts * BLOCK
    upper_row = lower_row + counts
    member = (positions[None, :] >= lower_row[:, None]) & (positions[None, :] < upper_row[:, None])
    masked = jnp.where(member[:, :, None], hidden.astype(jnp.float32)[None, :, :], 0.0)
    return jnp.einsum('rd,erf->edf', grads.astype(jnp.float32), masked)

def reference(saved_hidden, routed_grad, expert_counts, block_starts, master_weights, first_moment, second_moment):
    replicas = N_OUTER * N_REP
    row_total = N_EXP * CAP
    hidden_all = saved_hidden.reshape(replicas, N_EXP, row_total, FF)
    grads_all = routed_grad.reshape(replicas, N_EXP, N_EXP, CAP, D)
    counts_all = expert_counts.reshape(replicas, N_EXP, EXP_DEV)
    starts_all = block_starts.reshape(replicas, N_EXP, EXP_DEV)

    def group(owner):
        hidden_group = lax.dynamic_index_in_dim(hidden_all, owner, 1, keepdims=False)
        grads_group = lax.dynamic_index_in_dim(grads_all, owner, 2, keepdims=False).reshape(replicas, row_total, D)
        counts_group = lax.dynamic_index_in_dim(counts_all, owner, 1, keepdims=False)
        starts_group = lax.dynamic_index_in_dim(starts_all, owner, 1, keepdims=False)

        def add(summed, item):
            partial_value = device_partial(item[0], item[1], item[2], item[3])
            rounded = lax.optimization_barrier(partial_value.astype(jnp.bfloat16))
            return (summed + rounded.astype(jnp.float32), None)
        summed, unused = lax.scan(add, jnp.zeros((EXP_DEV, D, FF), jnp.float32), (hidden_group, grads_group, counts_group, starts_group))
        return summed
    grouped = lax.map(group, jnp.arange(N_EXP, dtype=jnp.int32))
    grad_full = grouped.reshape(N_EXP * EXP_DEV, D, FF)
    new_master, new_first, new_second = adamw(grad_full, master_weights, first_moment, second_moment)
    return (new_master, new_first, new_second, new_master.astype(jnp.bfloat16))
```

```python
import functools

import jax
import jax.numpy as jnp
from jax import lax
from jax.experimental import pallas as pl
from jax.experimental.pallas import tpu as pltpu
from jax.sharding import PartitionSpec as P

MESH = pl.DeviceIdType.MESH
BLOCK = 128
LANE = 128
SUB = 16
AHEAD = 2

beta_one = 0.9
beta_two = 0.95
learn_rate = 0.001
decay_rate = 0.1
epsilon = 1e-08
correct_one = 0.9999734386011124
correct_two = 0.994079470779666


def adamw(grad_part, master, moment_one, moment_two):
    new_one = beta_one * moment_one + (1.0 - beta_one) * grad_part
    new_two = beta_two * moment_two + (1.0 - beta_two) * grad_part * grad_part
    update = new_one / correct_one / (jnp.sqrt(new_two / correct_two) + epsilon)
    new_master = master - learn_rate * (update + decay_rate * master)
    return (new_master, new_one, new_two)


def kernel(
    n_y,
    n_z,
    counts_ref,
    starts_ref,
    hidden_hbm,
    grads_hbm,
    master_hbm,
    first_hbm,
    second_hbm,
    new_master,
    new_first,
    new_second,
    weights_hbm,
    grads,
    hidden,
    master,
    first,
    second,
    spread,
    outgoing,
    arrived,
    turned,
    partial,
    from_x,
    to_y,
    from_y,
    gathered,
    load_sem,
    turn_sem,
    z_send,
    z_recv,
    x_send,
    x_recv,
    y_send,
    y_recv,
    v_send,
    v_recv,
    u_send,
    u_recv,
    c_send,
    c_recv,
    out_sem,
):
    rows = grads.shape[0]
    slots = rows // n_z
    chunks = LANE // SUB
    outer = lax.axis_index("outer")
    rep = lax.axis_index("rep")
    z = lax.axis_index("exp")
    xh, c = outer // 2, outer % 2
    y, xl = rep // 2, rep % 2
    here = xh * 2 + xl

    def device(xh=xh, xl=xl, y=y, z=z, c=c):
        return (xh * 2 + c, y * 2 + xl, z)

    def push(src, dst, send_sem, recv_sem, target):
        pltpu.make_async_remote_copy(
            src_ref=src,
            dst_ref=dst,
            send_sem=send_sem,
            recv_sem=recv_sem,
            device_id=target,
            device_id_type=MESH,
        ).start()

    def take(like, sem):
        pltpu.make_async_copy(like, like, sem).wait()

    loads = [
        (grads_hbm.at[0, 0], grads),
        (hidden_hbm.at[0, 0], hidden),
        (master_hbm, master),
        (first_hbm, first),
        (second_hbm, second),
    ]
    for index, (src, dst) in enumerate(loads):
        pltpu.make_async_copy(src, dst, load_sem.at[index]).start()

    def loaded(index):
        pltpu.make_async_copy(*loads[index], load_sem.at[index]).wait()

    z_order = [n_z // 2]
    for step in range(n_z // 2 - 1, 0, -1):
        z_order += [step, n_z - step]
    barrier = pltpu.get_barrier_semaphore()
    peers = [device(z=lax.rem(z + dz, n_z), c=cc) for dz in z_order for cc in (0, 1)]
    peers += [device(c=1 - c)]
    peers += [
        device(xh=(xh + dh) % 2, xl=(xl + dl) % 2, c=cc)
        for dh, dl in ((0, 1), (1, 0), (1, 1))
        for cc in (0, 1)
    ]
    peers += [device(y=lax.rem(y + dy, n_y)) for dy in range(1, n_y)]
    for peer in peers:
        pl.semaphore_signal(barrier, inc=1, device_id=peer, device_id_type=MESH)

    row = lax.broadcasted_iota(jnp.int32, spread.shape, 0)
    lane = lax.broadcasted_iota(jnp.int32, spread.shape, 1)
    wanted = (lane % LANE) // SUB * (2 * LANE) + lane // LANE * LANE + lane % SUB
    spread[...] = jnp.where(row - (LANE - SUB) == wanted, 1.0, 0.0).astype(jnp.bfloat16)
    loaded(0)
    pl.semaphore_wait(barrier, len(peers))

    def send_grads(t):
        window = spread[pl.ds(pl.multiple_of((LANE - SUB) - SUB * t, SUB), grads.shape[1]), :]
        permuted = jnp.dot(grads[...], window, preferred_element_type=jnp.float32)
        permuted = permuted.astype(jnp.bfloat16)
        outgoing[t, 0] = permuted[:, :LANE]
        outgoing[t, 1] = permuted[:, LANE:]
        landing = pl.ds(pl.multiple_of(c * rows + z * slots, slots), slots)
        for dz in z_order:
            to = lax.rem(z + dz, n_z)
            leaving = pl.ds(pl.multiple_of(to * slots, slots), slots)
            for cc in (0, 1):
                push(
                    outgoing.at[t, cc, leaving],
                    arrived.at[t, landing],
                    z_send.at[t],
                    z_recv.at[t],
                    device(z=to, c=cc),
                )
        staying = pl.ds(pl.multiple_of(z * slots, slots), slots)
        push(
            outgoing.at[t, 1 - c, staying],
            arrived.at[t, landing],
            z_send.at[t],
            z_recv.at[t],
            device(c=1 - c),
        )
        pltpu.make_async_copy(
            outgoing.at[t, c, staying], arrived.at[t, landing], z_recv.at[t]
        ).start()

    def turn_hidden():
        loaded(1)
        position = lax.broadcasted_iota(jnp.int32, (LANE, rows), 1)
        for tile in range(4):
            flipped = hidden[:, tile * LANE : (tile + 1) * LANE].astype(jnp.float32).T
            for e in (0, 1):
                lower = starts_ref[0, 0, e] * BLOCK
                upper = lower + counts_ref[0, 0, e]
                kept = jnp.where((position >= lower) & (position < upper), flipped, 0.0)
                at = (tile * 2 + e) * LANE
                turned[c, at : at + LANE, :] = kept.astype(jnp.bfloat16)
        push(turned.at[c], turned.at[c], turn_sem.at[0], turn_sem.at[1], device(c=1 - c))
        for index in (2, 3, 4):
            loaded(index)
        take(turned.at[0], turn_sem.at[1])

    def multiply(t):
        take(arrived.at[t], z_recv.at[t])
        for piece in range(4):
            at = slice(piece * 2 * LANE, (piece + 1) * 2 * LANE)
            left = jnp.concatenate([turned[0, at, :], turned[1, at, :]], axis=1)
            product = jnp.dot(left, arrived[t], preferred_element_type=jnp.float32)
            partial[t, piece] = product.astype(jnp.bfloat16)
            th, tc = piece // 2, piece % 2
            mine = (xl == c) & (xh == th) & (c == tc)

            @pl.when(mine)
            def _():
                pltpu.make_async_copy(
                    partial.at[t, piece], from_x.at[t, here], x_recv.at[t]
                ).start()

            @pl.when(jnp.logical_not(mine))
            def _():
                push(
                    partial.at[t, piece],
                    from_x.at[t, here],
                    x_send.at[t],
                    x_recv.at[t],
                    device(xh=th, xl=c, c=tc),
                )

    def sum_x(t):
        take(from_x.at[t], x_recv.at[t])
        for e in (0, 1):
            at = slice(e * LANE, (e + 1) * LANE)
            total = from_x[t, 0, at, :].astype(jnp.float32)
            for source in range(1, 4):
                total += from_x[t, source, at, :].astype(jnp.float32)
            flat = total.T.astype(jnp.bfloat16)
            for to in range(n_y):
                to_y[t, to, e] = flat[to * SUB : (to + 1) * SUB, :]
        for dy in range(1, n_y):
            to = lax.rem(y + dy, n_y)
            push(to_y.at[t, to], from_y.at[t, y], y_send.at[t], y_recv.at[t], device(y=to))
        pltpu.make_async_copy(to_y.at[t, y], from_y.at[t, y], y_recv.at[t]).start()

    def update(t):
        take(from_y.at[t], y_recv.at[t])
        total = from_y[t, 0].astype(jnp.float32)
        for source in range(1, n_y):
            total += from_y[t, source].astype(jnp.float32)
        at = pl.ds(pl.multiple_of(t * SUB, SUB), SUB)
        one, two, three = adamw(total, master[:, at, :], first[:, at, :], second[:, at, :])
        new_master[:, at, :] = one
        new_first[:, at, :] = two
        new_second[:, at, :] = three
        gathered[t, c, here, :, y] = one.astype(jnp.bfloat16)
        block = gathered.at[t, c, here, :, y]
        for dy in range(1, n_y):
            push(block, block, v_send.at[t], v_recv.at[t], device(y=lax.rem(y + dy, n_y)))

    def gather_x(t):
        take(gathered.at[t, c, here, :, pl.ds(0, n_y - 1)], v_recv.at[t])
        block = gathered.at[t, c, here]
        for dh, dl in ((1, 1), (0, 1), (1, 0)):
            to = device(xh=(xh + dh) % 2, xl=(xl + dl) % 2)
            push(block, block, u_send.at[t], u_recv.at[t], to)

    def write_out(t, core):
        for tile in range(4):
            th, tl = tile // 2, tile % 2
            columns = pl.ds(pl.multiple_of((th * 2 + core) * LANE, LANE), LANE)
            pltpu.make_async_copy(
                gathered.at[t, core, tile],
                weights_hbm.at[:, :, tl, t, :, columns],
                out_sem.at[t],
            ).start()

    def cross(t):
        take(gathered.at[t, c, pl.ds(0, 3)], u_recv.at[t])
        block = gathered.at[t, c]
        push(block, block, c_send.at[t], c_recv.at[t], device(c=1 - c))
        write_out(t, c)

    def finish(t):
        take(gathered.at[t, c], c_recv.at[t])
        write_out(t, 1 - c)

    def at_step(s, delay, stage):
        @pl.when((s >= delay) & (s < delay + chunks))
        def _():
            stage((s + (2 * chunks - delay)) % chunks)

    def step(s, carry):
        at_step(s, 0, send_grads)

        @pl.when(s == AHEAD - 1)
        def _():
            turn_hidden()

        at_step(s, AHEAD, multiply)
        at_step(s, AHEAD + 1, update)
        at_step(s, AHEAD, sum_x)
        at_step(s, AHEAD + 2, cross)
        at_step(s, AHEAD + 1, gather_x)
        at_step(s, AHEAD + 2, finish)
        return carry

    lax.fori_loop(0, chunks + AHEAD + 2, step, 0)

    take(turned.at[0], turn_sem.at[0])

    def drain(t, carry):
        take(arrived.at[t, pl.ds(0, 2 * rows - slots)], z_send.at[t])

        @pl.when(xl == c)
        def _():
            take(from_x.at[t, pl.ds(0, 3)], x_send.at[t])

        @pl.when(xl != c)
        def _():
            take(from_x.at[t], x_send.at[t])

        take(from_y.at[t, pl.ds(0, n_y - 1)], y_send.at[t])
        take(from_y.at[t, pl.ds(0, n_y - 1)], v_send.at[t])
        take(gathered.at[t, c, pl.ds(0, 3)], u_send.at[t])
        take(gathered.at[t, c], c_send.at[t])
        take(gathered.at[t], out_sem.at[t])
        return carry

    lax.fori_loop(0, chunks, drain, 0)


def body(
    saved_hidden,
    routed_grad,
    expert_counts,
    block_starts,
    master_weights,
    first_moment,
    second_moment,
):
    rows, d = routed_grad.shape[2:]
    ff = saved_hidden.shape[3]
    n_y = lax.axis_size("rep") // 2
    n_z = lax.axis_size("exp")
    chunks = LANE // SUB
    shard = master_weights.shape
    bf16, f32 = jnp.bfloat16, jnp.float32
    smem = pl.BlockSpec(memory_space=pltpu.SMEM)
    vmem = pl.BlockSpec(memory_space=pltpu.VMEM)
    anywhere = pl.BlockSpec(memory_space=pl.ANY)
    sems = pltpu.SemaphoreType.DMA((chunks,))
    new_master, new_first, new_second, weights = pl.pallas_call(
        functools.partial(kernel, n_y, n_z),
        out_shape=[jax.ShapeDtypeStruct(shard, f32)] * 3
        + [jax.ShapeDtypeStruct((2, n_y, 2, chunks, SUB, ff), bf16)],
        in_specs=[smem, smem] + [anywhere] * 5,
        out_specs=[vmem] * 3 + [anywhere],
        scratch_shapes=[
            pltpu.VMEM((rows, d), bf16),
            pltpu.VMEM((rows, ff), bf16),
            pltpu.VMEM(shard, f32),
            pltpu.VMEM(shard, f32),
            pltpu.VMEM(shard, f32),
            pltpu.VMEM((d + LANE - SUB, 2 * LANE), bf16),
            pltpu.VMEM((chunks, 2, rows, LANE), bf16),
            pltpu.VMEM((chunks, 2 * rows, LANE), bf16),
            pltpu.VMEM((2, 2 * ff, rows), bf16),
            pltpu.VMEM((chunks, 4, 2 * LANE, LANE), bf16),
            pltpu.VMEM((chunks, 4, 2 * LANE, LANE), bf16),
            pltpu.VMEM((chunks, n_y, 2, SUB, LANE), bf16),
            pltpu.VMEM((chunks, n_y, 2, SUB, LANE), bf16),
            pltpu.VMEM((chunks, 2, 4, 2, n_y, SUB, LANE), bf16),
            pltpu.SemaphoreType.DMA((5,)),
            pltpu.SemaphoreType.DMA((2,)),
        ]
        + [sems] * 13,
        compiler_params=pltpu.CompilerParams(
            collective_id=0, has_side_effects=True, vmem_limit_bytes=40 << 20
        ),
        name="expert_update",
    )(
        expert_counts,
        block_starts,
        saved_hidden,
        routed_grad,
        master_weights,
        first_moment,
        second_moment,
    )
    return (new_master, new_first, new_second, weights.reshape(2, d, ff))


def solution(mesh):
    in_specs = (
        P("outer", "rep", "exp", None),
        P("outer", "rep", "exp", None),
        P("outer", "rep", "exp"),
        P("outer", "rep", "exp"),
        P("exp", "rep", "outer"),
        P("exp", "rep", "outer"),
        P("exp", "rep", "outer"),
    )
    out_specs = (
        P("exp", "rep", "outer"),
        P("exp", "rep", "outer"),
        P("exp", "rep", "outer"),
        P("exp", None, None),
    )
    return jax.shard_map(body, mesh=mesh, in_specs=in_specs, out_specs=out_specs, check_vma=False)
```

```python
import functools

import jax
import jax.numpy as jnp
from jax import lax
from jax.experimental import pallas as pl
from jax.experimental.pallas import tpu as pltpu
from jax.sharding import PartitionSpec as P

MESH = pl.DeviceIdType.MESH
BLOCK = 128
LANE = 128
SUB = 16
AHEAD = 2

beta_one = 0.9
beta_two = 0.95
learn_rate = 0.001
decay_rate = 0.1
epsilon = 1e-08
correct_one = 0.9999734386011124
correct_two = 0.994079470779666


def adamw(grad_part, master, moment_one, moment_two):
    new_one = beta_one * moment_one + (1.0 - beta_one) * grad_part
    new_two = beta_two * moment_two + (1.0 - beta_two) * grad_part * grad_part
    update = new_one / correct_one / (jnp.sqrt(new_two / correct_two) + epsilon)
    new_master = master - learn_rate * (update + decay_rate * master)
    return (new_master, new_one, new_two)


def kernel(
    n_y,
    n_z,
    counts_hbm,
    starts_hbm,
    hidden_hbm,
    grads_hbm,
    master_hbm,
    first_hbm,
    second_hbm,
    new_master,
    new_first,
    new_second,
    gathered,
    counts,
    starts,
    grads,
    hidden,
    master,
    first,
    second,
    spread,
    outgoing,
    arrived,
    turned,
    partial,
    from_x,
    to_y,
    from_y,
    load_sem,
    turn_sem,
    z_send,
    z_recv,
    x_send,
    x_recv,
    y_send,
    y_recv,
    y_first_send,
    y_first_recv,
    x_first_send,
    x_first_recv,
    x_last_send,
    x_last_recv,
    y_last_send,
    y_last_recv,
    c_send,
    c_recv,
):
    rows = grads.shape[0]
    slots = rows // n_z
    chunks = LANE // SUB
    outer = lax.axis_index("outer")
    rep = lax.axis_index("rep")
    z = lax.axis_index("exp")
    xh, c = outer // 2, outer % 2
    y, xl = rep // 2, rep % 2
    here = xh * 2 + xl

    def device(xh=xh, xl=xl, y=y, z=z, c=c):
        return (xh * 2 + c, y * 2 + xl, z)

    def push(src, dst, send_sem, recv_sem, target):
        pltpu.make_async_remote_copy(
            src_ref=src,
            dst_ref=dst,
            send_sem=send_sem,
            recv_sem=recv_sem,
            device_id=target,
            device_id_type=MESH,
        ).start()

    def take(like, sem):
        pltpu.make_async_copy(like, like, sem).wait()

    loads = [
        (grads_hbm.at[0, 0], grads),
        (hidden_hbm.at[0, 0], hidden),
        (master_hbm, master),
        (first_hbm, first),
        (second_hbm, second),
        (counts_hbm, counts),
        (starts_hbm, starts),
    ]
    for index, (src, dst) in enumerate(loads):
        pltpu.make_async_copy(src, dst, load_sem.at[index]).start()

    def loaded(index):
        pltpu.make_async_copy(*loads[index], load_sem.at[index]).wait()

    y_peers = [device(y=lax.rem(y + dy, n_y)) for dy in range(1, n_y)]
    x_peers = [
        device(xh=(xh + dh) % 2, xl=(xl + dl) % 2) for dh, dl in ((1, 1), (0, 1), (1, 0))
    ]
    z_order = [n_z // 2]
    for step in range(n_z // 2 - 1, 0, -1):
        z_order += [step, n_z - step]
    barrier = pltpu.get_barrier_semaphore()
    peers = [device(z=lax.rem(z + dz, n_z), c=cc) for dz in z_order for cc in (0, 1)]
    peers += [device(c=1 - c)]
    peers += [
        device(xh=(xh + dh) % 2, xl=(xl + dl) % 2, c=cc)
        for dh, dl in ((0, 1), (1, 0), (1, 1))
        for cc in (0, 1)
    ]
    peers += y_peers
    for peer in peers:
        pl.semaphore_signal(barrier, inc=1, device_id=peer, device_id_type=MESH)

    row = lax.broadcasted_iota(jnp.int32, spread.shape, 0)
    lane = lax.broadcasted_iota(jnp.int32, (1, spread.shape[1]), 1)
    wanted = (LANE - SUB) + (lane % LANE) // SUB * (2 * LANE) + lane // LANE * LANE + lane % SUB
    spread[...] = jnp.where(row == wanted, 1.0, 0.0).astype(jnp.bfloat16)
    loaded(0)
    pl.semaphore_wait(barrier, len(peers))

    def send_grads(t):
        window = spread[pl.ds(pl.multiple_of((LANE - SUB) - SUB * t, SUB), grads.shape[1]), :]
        permuted = jnp.dot(grads[...], window, preferred_element_type=jnp.float32)
        permuted = permuted.astype(jnp.bfloat16)
        outgoing[t, 0] = permuted[:, :LANE]
        outgoing[t, 1] = permuted[:, LANE:]
        landing = pl.ds(pl.multiple_of(c * rows + z * slots, slots), slots)
        for dz in z_order:
            to = lax.rem(z + dz, n_z)
            leaving = pl.ds(pl.multiple_of(to * slots, slots), slots)
            for cc in (0, 1):
                push(
                    outgoing.at[t, cc, leaving],
                    arrived.at[t, landing],
                    z_send.at[t],
                    z_recv.at[t],
                    device(z=to, c=cc),
                )
        staying = pl.ds(pl.multiple_of(z * slots, slots), slots)
        push(
            outgoing.at[t, 1 - c, staying],
            arrived.at[t, landing],
            z_send.at[t],
            z_recv.at[t],
            device(c=1 - c),
        )
        pltpu.make_async_copy(
            outgoing.at[t, c, staying], arrived.at[t, landing], z_recv.at[t]
        ).start()

    def turn_hidden():
        for index in (1, 5, 6):
            loaded(index)
        position = lax.broadcasted_iota(jnp.int32, (LANE, rows), 1)
        for tile in range(4):
            flipped = hidden[:, tile * LANE : (tile + 1) * LANE].astype(jnp.float32).T
            for e in (0, 1):
                lower = starts[0, :, e : e + 1] * BLOCK
                upper = lower + counts[0, :, e : e + 1]
                kept = jnp.where((position >= lower) & (position < upper), flipped, 0.0)
                at = (tile * 2 + e) * LANE
                turned[c, at : at + LANE, :] = kept.astype(jnp.bfloat16)
        push(turned.at[c], turned.at[c], turn_sem.at[0], turn_sem.at[1], device(c=1 - c))
        for index in (2, 3, 4):
            loaded(index)
        take(turned.at[0], turn_sem.at[1])

    def multiply(t):
        take(arrived.at[t], z_recv.at[t])
        for piece in range(4):
            at = slice(piece * 2 * LANE, (piece + 1) * 2 * LANE)
            left = jnp.concatenate([turned[0, at, :], turned[1, at, :]], axis=1)
            product = jnp.dot(left, arrived[t], preferred_element_type=jnp.float32)
            partial[t, piece] = product.astype(jnp.bfloat16)
            th, tc = piece // 2, piece % 2
            mine = (xl == c) & (xh == th) & (c == tc)

            @pl.when(mine)
            def _():
                pltpu.make_async_copy(
                    partial.at[t, piece], from_x.at[t, here], x_recv.at[t]
                ).start()

            @pl.when(jnp.logical_not(mine))
            def _():
                push(
                    partial.at[t, piece],
                    from_x.at[t, here],
                    x_send.at[t],
                    x_recv.at[t],
                    device(xh=th, xl=c, c=tc),
                )

    def sum_x(t):
        take(from_x.at[t], x_recv.at[t])
        for e in (0, 1):
            at = slice(e * LANE, (e + 1) * LANE)
            total = from_x[t, 0, at, :].astype(jnp.float32)
            for source in range(1, 4):
                total += from_x[t, source, at, :].astype(jnp.float32)
            flat = total.T.astype(jnp.bfloat16)
            for to in range(n_y):
                to_y[t, to, e] = flat[to * SUB : (to + 1) * SUB, :]
        for dy in range(1, n_y):
            to = lax.rem(y + dy, n_y)
            push(to_y.at[t, to], from_y.at[t, y], y_send.at[t], y_recv.at[t], device(y=to))
        pltpu.make_async_copy(to_y.at[t, y], from_y.at[t, y], y_recv.at[t]).start()

    def update(t):
        take(from_y.at[t], y_recv.at[t])
        total = from_y[t, 0].astype(jnp.float32)
        for source in range(1, n_y):
            total += from_y[t, source].astype(jnp.float32)
        at = pl.ds(pl.multiple_of(t * SUB, SUB), SUB)
        one, two, three = adamw(total, master[:, at, :], first[:, at, :], second[:, at, :])
        new_master[:, at, :] = one
        new_first[:, at, :] = two
        new_second[:, at, :] = three
        for e in (0, 1):
            gathered[c, here, e, y, t] = one[e].astype(jnp.bfloat16)
        along_y = gathered.at[c, here, 0, y, t]
        along_x = gathered.at[c, here, 1, y, t]
        for to in y_peers:
            push(along_y, along_y, y_first_send.at[t], y_first_recv.at[t], to)
        for to in x_peers:
            push(along_x, along_x, x_first_send.at[t], x_first_recv.at[t], to)

    def gather(t):
        take(gathered.at[c, here, 0, pl.ds(0, n_y - 1), t], y_first_recv.at[t])
        along_x = gathered.at[c, here, 0, :, t]
        for to in x_peers:
            push(along_x, along_x, x_last_send.at[t], x_last_recv.at[t], to)
        take(gathered.at[c, pl.ds(0, 3), 1, y, t], x_first_recv.at[t])
        along_y = gathered.at[c, :, 1, y, t]
        for to in y_peers:
            push(along_y, along_y, y_last_send.at[t], y_last_recv.at[t], to)

    def cross(t):
        take(gathered.at[c, pl.ds(0, 3), 0, :, t], x_last_recv.at[t])
        take(gathered.at[c, :, 1, pl.ds(0, n_y - 1), t], y_last_recv.at[t])
        block = gathered.at[c, :, :, :, t]
        push(block, block, c_send.at[t], c_recv.at[t], device(c=1 - c))

    def at_step(s, delay, stage):
        @pl.when((s >= delay) & (s < delay + chunks))
        def _():
            stage((s + (2 * chunks - delay)) % chunks)

    def step(s, carry):
        at_step(s, AHEAD, multiply)
        at_step(s, 0, send_grads)

        @pl.when(s == AHEAD - 1)
        def _():
            turn_hidden()

        at_step(s, AHEAD + 1, sum_x)
        at_step(s, AHEAD + 2, update)
        at_step(s, AHEAD + 3, gather)
        at_step(s, AHEAD + 4, cross)
        return carry

    lax.fori_loop(0, chunks + AHEAD + 4, step, 0)

    take(turned.at[0], turn_sem.at[0])

    def drain(t, carry):
        take(arrived.at[t, pl.ds(0, 2 * rows - slots)], z_send.at[t])

        @pl.when(xl == c)
        def _():
            take(from_x.at[t, pl.ds(0, 3)], x_send.at[t])

        @pl.when(xl != c)
        def _():
            take(from_x.at[t], x_send.at[t])

        take(from_y.at[t, pl.ds(0, n_y - 1)], y_send.at[t])
        take(gathered.at[c, here, 0, pl.ds(0, n_y - 1), t], y_first_send.at[t])
        take(gathered.at[c, pl.ds(0, 3), 1, y, t], x_first_send.at[t])
        take(gathered.at[c, pl.ds(0, 3), 0, :, t], x_last_send.at[t])
        take(gathered.at[c, :, 1, pl.ds(0, n_y - 1), t], y_last_send.at[t])
        take(gathered.at[c, :, :, :, t], c_send.at[t])
        take(gathered.at[c, :, :, :, t], c_recv.at[t])
        return carry

    lax.fori_loop(0, chunks, drain, 0)


def write_kernel(master, first, second, gathered, master_out, first_out, second_out, weights, sem):
    copies = []
    for core in (0, 1):
        for tile in range(4):
            th, tl = tile // 2, tile % 2
            at = (th * 2 + core) * LANE
            copies.append((gathered.at[core, tile], weights.at[:, :, tl, :, :, at : at + LANE]))
    copies += [(master, master_out), (first, first_out), (second, second_out)]
    started = [
        pltpu.make_async_copy(src, dst, sem.at[index])
        for index, (src, dst) in enumerate(copies)
    ]
    for copy in started:
        copy.start()
    for copy in started:
        copy.wait()


def body(
    saved_hidden,
    routed_grad,
    expert_counts,
    block_starts,
    master_weights,
    first_moment,
    second_moment,
):
    rows, d = routed_grad.shape[2:]
    ff = saved_hidden.shape[3]
    n_y = lax.axis_size("rep") // 2
    n_z = lax.axis_size("exp")
    chunks = LANE // SUB
    shard = master_weights.shape
    bf16, f32 = jnp.bfloat16, jnp.float32
    vmem = pl.BlockSpec(memory_space=pltpu.VMEM)
    hbm = pl.BlockSpec(memory_space=pltpu.HBM)
    sems = pltpu.SemaphoreType.DMA((chunks,))
    shards = [jax.ShapeDtypeStruct(shard, f32)] * 3
    results = pl.pallas_call(
        functools.partial(kernel, n_y, n_z),
        out_shape=shards + [jax.ShapeDtypeStruct((2, 4, 2, n_y, chunks, SUB, LANE), bf16)],
        in_specs=[hbm] * 7,
        out_specs=[vmem] * 4,
        scratch_shapes=[
            pltpu.VMEM(expert_counts.shape, jnp.int32),
            pltpu.VMEM(block_starts.shape, jnp.int32),
            pltpu.VMEM((rows, d), bf16),
            pltpu.VMEM((rows, ff), bf16),
            pltpu.VMEM(shard, f32),
            pltpu.VMEM(shard, f32),
            pltpu.VMEM(shard, f32),
            pltpu.VMEM((d + LANE - SUB, 2 * LANE), bf16),
            pltpu.VMEM((chunks, 2, rows, LANE), bf16),
            pltpu.VMEM((chunks, 2 * rows, LANE), bf16),
            pltpu.VMEM((2, 2 * ff, rows), bf16),
            pltpu.VMEM((chunks, 4, 2 * LANE, LANE), bf16),
            pltpu.VMEM((chunks, 4, 2 * LANE, LANE), bf16),
            pltpu.VMEM((chunks, n_y, 2, SUB, LANE), bf16),
            pltpu.VMEM((chunks, n_y, 2, SUB, LANE), bf16),
            pltpu.SemaphoreType.DMA((7,)),
            pltpu.SemaphoreType.DMA((2,)),
        ]
        + [sems] * 16,
        compiler_params=pltpu.CompilerParams(
            collective_id=0, has_side_effects=True, vmem_limit_bytes=40 << 20
        ),
        name="expert_update",
    )(
        pltpu.with_memory_space_constraint(expert_counts, pltpu.HBM),
        pltpu.with_memory_space_constraint(block_starts, pltpu.HBM),
        pltpu.with_memory_space_constraint(saved_hidden, pltpu.HBM),
        pltpu.with_memory_space_constraint(routed_grad, pltpu.HBM),
        pltpu.with_memory_space_constraint(master_weights, pltpu.HBM),
        pltpu.with_memory_space_constraint(first_moment, pltpu.HBM),
        pltpu.with_memory_space_constraint(second_moment, pltpu.HBM),
    )
    new_master, new_first, new_second, weights = pl.pallas_call(
        write_kernel,
        out_shape=shards + [jax.ShapeDtypeStruct((2, n_y, 2, chunks, SUB, ff), bf16)],
        in_specs=[vmem] * 4,
        out_specs=[hbm] * 4,
        scratch_shapes=[pltpu.SemaphoreType.DMA((11,))],
        compiler_params=pltpu.CompilerParams(vmem_limit_bytes=16 << 20),
        name="write_results",
    )(*results)
    return (new_master, new_first, new_second, weights.reshape(2, d, ff))


def solution(mesh):
    in_specs = (
        P("outer", "rep", "exp", None),
        P("outer", "rep", "exp", None),
        P("outer", "rep", "exp"),
        P("outer", "rep", "exp"),
        P("exp", "rep", "outer"),
        P("exp", "rep", "outer"),
        P("exp", "rep", "outer"),
    )
    out_specs = (
        P("exp", "rep", "outer"),
        P("exp", "rep", "outer"),
        P("exp", "rep", "outer"),
        P("exp", None, None),
    )
    return jax.shard_map(body, mesh=mesh, in_specs=in_specs, out_specs=out_specs, check_vma=False)
```

```python
import functools

import jax
import jax.numpy as jnp
from jax import lax
from jax.experimental import pallas as pl
from jax.experimental.pallas import tpu as pltpu
from jax.sharding import PartitionSpec as P

MESH = pl.DeviceIdType.MESH
BLOCK = 128
LANE = 128
SUB = 16
AHEAD = 4

beta_one = 0.9
beta_two = 0.95
learn_rate = 0.001
decay_rate = 0.1
epsilon = 1e-08
correct_one = 0.9999734386011124
correct_two = 0.994079470779666


def adamw(grad_part, master, moment_one, moment_two):
    new_one = beta_one * moment_one + (1.0 - beta_one) * grad_part
    new_two = beta_two * moment_two + (1.0 - beta_two) * grad_part * grad_part
    update = new_one / correct_one / (jnp.sqrt(new_two / correct_two) + epsilon)
    new_master = master - learn_rate * (update + decay_rate * master)
    return (new_master, new_one, new_two)


def kernel(
    n_y,
    n_z,
    counts_hbm,
    starts_hbm,
    hidden_hbm,
    grads_hbm,
    master_hbm,
    first_hbm,
    second_hbm,
    new_master,
    new_first,
    new_second,
    gathered,
    counts,
    starts,
    grads,
    hidden,
    master,
    first,
    second,
    spread,
    outgoing,
    arrived,
    turned,
    partial,
    from_x,
    to_y,
    from_y,
    load_sem,
    turn_sem,
    z_send,
    z_recv,
    x_send,
    x_recv,
    y_send,
    y_recv,
    y_first_send,
    y_first_recv,
    x_first_send,
    x_first_recv,
    x_last_send,
    x_last_recv,
    y_last_send,
    y_last_recv,
    c_send,
    c_recv,
):
    rows = grads.shape[0]
    slots = rows // n_z
    chunks = LANE // SUB
    outer = lax.axis_index("outer")
    rep = lax.axis_index("rep")
    z = lax.axis_index("exp")
    xh, c = outer // 2, outer % 2
    y, xl = rep // 2, rep % 2
    here = xh * 2 + xl

    def device(xh=xh, xl=xl, y=y, z=z, c=c):
        return (xh * 2 + c, y * 2 + xl, z)

    def push(src, dst, send_sem, recv_sem, target):
        pltpu.make_async_remote_copy(
            src_ref=src,
            dst_ref=dst,
            send_sem=send_sem,
            recv_sem=recv_sem,
            device_id=target,
            device_id_type=MESH,
        ).start()

    def take(like, sem):
        pltpu.make_async_copy(like, like, sem).wait()

    loads = [
        (grads_hbm.at[0, 0], grads),
        (hidden_hbm.at[0, 0], hidden),
        (master_hbm, master),
        (first_hbm, first),
        (second_hbm, second),
        (counts_hbm, counts),
        (starts_hbm, starts),
    ]
    for index, (src, dst) in enumerate(loads):
        pltpu.make_async_copy(src, dst, load_sem.at[index]).start()

    def loaded(index):
        pltpu.make_async_copy(*loads[index], load_sem.at[index]).wait()

    y_peers = [device(y=lax.rem(y + dy, n_y)) for dy in range(1, n_y)]
    x_peers = [
        device(xh=(xh + dh) % 2, xl=(xl + dl) % 2) for dh, dl in ((1, 1), (0, 1), (1, 0))
    ]
    z_order = [n_z // 2]
    for step in range(n_z // 2 - 1, 0, -1):
        z_order += [step, n_z - step]
    barrier = pltpu.get_barrier_semaphore()
    peers = [device(z=lax.rem(z + dz, n_z), c=cc) for dz in z_order for cc in (0, 1)]
    peers += [device(c=1 - c)]
    peers += [
        device(xh=(xh + dh) % 2, xl=(xl + dl) % 2, c=cc)
        for dh, dl in ((0, 1), (1, 0), (1, 1))
        for cc in (0, 1)
    ]
    peers += y_peers
    for peer in peers:
        pl.semaphore_signal(barrier, inc=1, device_id=peer, device_id_type=MESH)

    row = lax.broadcasted_iota(jnp.int32, spread.shape, 0)
    lane = lax.broadcasted_iota(jnp.int32, (1, spread.shape[1]), 1)
    wanted = (LANE - SUB) + (lane % LANE) // SUB * (2 * LANE) + lane // LANE * LANE + lane % SUB
    spread[...] = jnp.where(row == wanted, 1.0, 0.0).astype(jnp.bfloat16)

    def permute(t):
        window = spread[pl.ds(pl.multiple_of((LANE - SUB) - SUB * t, SUB), grads.shape[1]), :]
        permuted = jnp.dot(grads[...], window, preferred_element_type=jnp.float32)
        permuted = permuted.astype(jnp.bfloat16)
        outgoing[t, 0] = permuted[:, :LANE]
        outgoing[t, 1] = permuted[:, LANE:]

    loaded(0)
    permute(0)
    pl.semaphore_wait(barrier, len(peers))

    def send_grads(t):
        landing = pl.ds(pl.multiple_of(c * rows + z * slots, slots), slots)
        for dz in z_order:
            to = lax.rem(z + dz, n_z)
            leaving = pl.ds(pl.multiple_of(to * slots, slots), slots)
            for cc in (0, 1):
                push(
                    outgoing.at[t, cc, leaving],
                    arrived.at[t, landing],
                    z_send.at[t],
                    z_recv.at[t],
                    device(z=to, c=cc),
                )
        staying = pl.ds(pl.multiple_of(z * slots, slots), slots)
        push(
            outgoing.at[t, 1 - c, staying],
            arrived.at[t, landing],
            z_send.at[t],
            z_recv.at[t],
            device(c=1 - c),
        )
        pltpu.make_async_copy(
            outgoing.at[t, c, staying], arrived.at[t, landing], z_recv.at[t]
        ).start()

    def turn_hidden():
        for index in (1, 5, 6):
            loaded(index)
        position = lax.broadcasted_iota(jnp.int32, (LANE, rows), 1)
        for tile in range(4):
            flipped = hidden[:, tile * LANE : (tile + 1) * LANE].astype(jnp.float32).T
            for e in (0, 1):
                lower = starts[0, :, e : e + 1] * BLOCK
                upper = lower + counts[0, :, e : e + 1]
                kept = jnp.where((position >= lower) & (position < upper), flipped, 0.0)
                at = (tile * 2 + e) * LANE
                turned[c, at : at + LANE, :] = kept.astype(jnp.bfloat16)
        push(turned.at[c], turned.at[c], turn_sem.at[0], turn_sem.at[1], device(c=1 - c))
        for index in (2, 3, 4):
            loaded(index)
        take(turned.at[0], turn_sem.at[1])

    def multiply(t):
        take(arrived.at[t], z_recv.at[t])
        for piece in range(4):
            at = slice(piece * 2 * LANE, (piece + 1) * 2 * LANE)
            left = jnp.concatenate([turned[0, at, :], turned[1, at, :]], axis=1)
            product = jnp.dot(left, arrived[t], preferred_element_type=jnp.float32)
            partial[t, piece] = product.astype(jnp.bfloat16)
            th, tc = piece // 2, piece % 2
            mine = (xl == c) & (xh == th) & (c == tc)

            @pl.when(mine)
            def _():
                pltpu.make_async_copy(
                    partial.at[t, piece], from_x.at[t, here], x_recv.at[t]
                ).start()

            @pl.when(jnp.logical_not(mine))
            def _():
                push(
                    partial.at[t, piece],
                    from_x.at[t, here],
                    x_send.at[t],
                    x_recv.at[t],
                    device(xh=th, xl=c, c=tc),
                )

    def sum_x(t):
        take(from_x.at[t], x_recv.at[t])
        for e in (0, 1):
            at = slice(e * LANE, (e + 1) * LANE)
            total = from_x[t, 0, at, :].astype(jnp.float32)
            for source in range(1, 4):
                total += from_x[t, source, at, :].astype(jnp.float32)
            flat = total.T.astype(jnp.bfloat16)
            for to in range(n_y):
                to_y[t, to, e] = flat[to * SUB : (to + 1) * SUB, :]
        for dy in range(1, n_y):
            to = lax.rem(y + dy, n_y)
            push(to_y.at[t, to], from_y.at[t, y], y_send.at[t], y_recv.at[t], device(y=to))
        pltpu.make_async_copy(to_y.at[t, y], from_y.at[t, y], y_recv.at[t]).start()

    def update(t):
        take(from_y.at[t], y_recv.at[t])
        total = from_y[t, 0].astype(jnp.float32)
        for source in range(1, n_y):
            total += from_y[t, source].astype(jnp.float32)
        at = pl.ds(pl.multiple_of(t * SUB, SUB), SUB)
        one, two, three = adamw(total, master[:, at, :], first[:, at, :], second[:, at, :])
        new_master[:, at, :] = one
        new_first[:, at, :] = two
        new_second[:, at, :] = three
        for e in (0, 1):
            gathered[c, here, e, y, t] = one[e].astype(jnp.bfloat16)
        along_y = gathered.at[c, here, 0, y, t]
        along_x = gathered.at[c, here, 1, y, t]
        for to in y_peers:
            push(along_y, along_y, y_first_send.at[t], y_first_recv.at[t], to)
        for to in x_peers:
            push(along_x, along_x, x_first_send.at[t], x_first_recv.at[t], to)

    def gather(t):
        take(gathered.at[c, here, 0, pl.ds(0, n_y - 1), t], y_first_recv.at[t])
        along_x = gathered.at[c, here, 0, :, t]
        for to in x_peers:
            push(along_x, along_x, x_last_send.at[t], x_last_recv.at[t], to)
        take(gathered.at[c, pl.ds(0, 3), 1, y, t], x_first_recv.at[t])
        along_y = gathered.at[c, :, 1, y, t]
        for to in y_peers:
            push(along_y, along_y, y_last_send.at[t], y_last_recv.at[t], to)

    def cross(t):
        take(gathered.at[c, pl.ds(0, 3), 0, :, t], x_last_recv.at[t])
        take(gathered.at[c, :, 1, pl.ds(0, n_y - 1), t], y_last_recv.at[t])
        block = gathered.at[c, :, :, :, t]
        push(block, block, c_send.at[t], c_recv.at[t], device(c=1 - c))

    def at_step(s, delay, stage):
        @pl.when((s >= delay) & (s < delay + chunks))
        def _():
            stage((s + (2 * chunks - delay)) % chunks)

    def step(s, carry):
        at_step(s, AHEAD, multiply)
        at_step(s, 0, send_grads)

        @pl.when(s < chunks - 1)
        def _():
            permute((s + 1) % chunks)

        @pl.when(s == AHEAD - 1)
        def _():
            turn_hidden()

        at_step(s, AHEAD + 1, sum_x)
        at_step(s, AHEAD + 2, update)
        at_step(s, AHEAD + 3, gather)
        at_step(s, AHEAD + 5, cross)
        return carry

    lax.fori_loop(0, chunks + AHEAD + 5, step, 0)

    take(turned.at[0], turn_sem.at[0])

    def drain(t, carry):
        take(arrived.at[t, pl.ds(0, 2 * rows - slots)], z_send.at[t])

        @pl.when(xl == c)
        def _():
            take(from_x.at[t, pl.ds(0, 3)], x_send.at[t])

        @pl.when(xl != c)
        def _():
            take(from_x.at[t], x_send.at[t])

        take(from_y.at[t, pl.ds(0, n_y - 1)], y_send.at[t])
        take(gathered.at[c, here, 0, pl.ds(0, n_y - 1), t], y_first_send.at[t])
        take(gathered.at[c, pl.ds(0, 3), 1, y, t], x_first_send.at[t])
        take(gathered.at[c, pl.ds(0, 3), 0, :, t], x_last_send.at[t])
        take(gathered.at[c, :, 1, pl.ds(0, n_y - 1), t], y_last_send.at[t])
        take(gathered.at[c, :, :, :, t], c_send.at[t])
        take(gathered.at[c, :, :, :, t], c_recv.at[t])
        return carry

    lax.fori_loop(0, chunks, drain, 0)


def write_kernel(master, first, second, gathered, master_out, first_out, second_out, weights, sem):
    copies = []
    for core in (0, 1):
        for tile in range(4):
            th, tl = tile // 2, tile % 2
            at = (th * 2 + core) * LANE
            copies.append((gathered.at[core, tile], weights.at[:, :, tl, :, :, at : at + LANE]))
    copies += [(master, master_out), (first, first_out), (second, second_out)]
    started = [
        pltpu.make_async_copy(src, dst, sem.at[index])
        for index, (src, dst) in enumerate(copies)
    ]
    for copy in started:
        copy.start()
    for copy in started:
        copy.wait()


def body(
    saved_hidden,
    routed_grad,
    expert_counts,
    block_starts,
    master_weights,
    first_moment,
    second_moment,
):
    rows, d = routed_grad.shape[2:]
    ff = saved_hidden.shape[3]
    n_y = lax.axis_size("rep") // 2
    n_z = lax.axis_size("exp")
    chunks = LANE // SUB
    shard = master_weights.shape
    bf16, f32 = jnp.bfloat16, jnp.float32
    vmem = pl.BlockSpec(memory_space=pltpu.VMEM)
    hbm = pl.BlockSpec(memory_space=pltpu.HBM)
    sems = pltpu.SemaphoreType.DMA((chunks,))
    shards = [jax.ShapeDtypeStruct(shard, f32)] * 3
    results = pl.pallas_call(
        functools.partial(kernel, n_y, n_z),
        out_shape=shards + [jax.ShapeDtypeStruct((2, 4, 2, n_y, chunks, SUB, LANE), bf16)],
        in_specs=[hbm] * 7,
        out_specs=[vmem] * 4,
        scratch_shapes=[
            pltpu.VMEM(expert_counts.shape, jnp.int32),
            pltpu.VMEM(block_starts.shape, jnp.int32),
            pltpu.VMEM((rows, d), bf16),
            pltpu.VMEM((rows, ff), bf16),
            pltpu.VMEM(shard, f32),
            pltpu.VMEM(shard, f32),
            pltpu.VMEM(shard, f32),
            pltpu.VMEM((d + LANE - SUB, 2 * LANE), bf16),
            pltpu.VMEM((chunks, 2, rows, LANE), bf16),
            pltpu.VMEM((chunks, 2 * rows, LANE), bf16),
            pltpu.VMEM((2, 2 * ff, rows), bf16),
            pltpu.VMEM((chunks, 4, 2 * LANE, LANE), bf16),
            pltpu.VMEM((chunks, 4, 2 * LANE, LANE), bf16),
            pltpu.VMEM((chunks, n_y, 2, SUB, LANE), bf16),
            pltpu.VMEM((chunks, n_y, 2, SUB, LANE), bf16),
            pltpu.SemaphoreType.DMA((7,)),
            pltpu.SemaphoreType.DMA((2,)),
        ]
        + [sems] * 16,
        compiler_params=pltpu.CompilerParams(
            collective_id=0, has_side_effects=True, vmem_limit_bytes=40 << 20
        ),
        name="expert_update",
    )(
        pltpu.with_memory_space_constraint(expert_counts, pltpu.HBM),
        pltpu.with_memory_space_constraint(block_starts, pltpu.HBM),
        pltpu.with_memory_space_constraint(saved_hidden, pltpu.HBM),
        pltpu.with_memory_space_constraint(routed_grad, pltpu.HBM),
        pltpu.with_memory_space_constraint(master_weights, pltpu.HBM),
        pltpu.with_memory_space_constraint(first_moment, pltpu.HBM),
        pltpu.with_memory_space_constraint(second_moment, pltpu.HBM),
    )
    new_master, new_first, new_second, weights = pl.pallas_call(
        write_kernel,
        out_shape=shards + [jax.ShapeDtypeStruct((2, n_y, 2, chunks, SUB, ff), bf16)],
        in_specs=[vmem] * 4,
        out_specs=[hbm] * 4,
        scratch_shapes=[pltpu.SemaphoreType.DMA((11,))],
        compiler_params=pltpu.CompilerParams(vmem_limit_bytes=16 << 20),
        name="write_results",
    )(*results)
    return (new_master, new_first, new_second, weights.reshape(2, d, ff))


def solution(mesh):
    in_specs = (
        P("outer", "rep", "exp", None),
        P("outer", "rep", "exp", None),
        P("outer", "rep", "exp"),
        P("outer", "rep", "exp"),
        P("exp", "rep", "outer"),
        P("exp", "rep", "outer"),
        P("exp", "rep", "outer"),
    )
    out_specs = (
        P("exp", "rep", "outer"),
        P("exp", "rep", "outer"),
        P("exp", "rep", "outer"),
        P("exp", None, None),
    )
    return jax.shard_map(body, mesh=mesh, in_specs=in_specs, out_specs=out_specs, check_vma=False)
```
